256 devices in a mesh: row: 16 (over y, x_lo, core), col: 16 (over z, x_hi).
Axes of the slice: x: 4 (x_hi: 2, x_lo: 2; x = x_hi * 2 + x_lo), y: 4, z: 8, core: 2. Of those that a mesh axis runs over, the one named last changes fastest.
Arguments:
- row_coefs: bfloat16 [14336, 16, 128], P('row', 'col'), may hold values from -8 to 8
- col_coefs: bfloat16 [14336, 16, 128], P('col', 'row'), may hold values from -8 to 8
- row_wedge: int32 [14336], P('row'), may hold values from 3 to 8
- col_wedge: int32 [14336], P('col'), may hold values from 3 to 8
- rotation: int32 [1], replicated, may hold values from 0 to 63
- best_in: float32 [14336, 14336], P('row', 'col'), may hold values from -0.3 to 0.5
Outputs:
- best_out: float32 [14336, 14336], P('row', 'col')
The draws below stay inside these ranges and needn't reach their ends.
All inputs are finite; a program needn't handle non-finite values.
Results may differ from the reference program's by a relative error of at most 0.0015.
Values may be sent and summed in bfloat16 or wider, within the bound.
No kernel may reach another device: no remote copies, remote signals or barrier semaphores. Data moves between devices by JAX's collectives and lax.ppermute only.
A program may use at most 64 MiB of HBM per device.

```python
import jax
import jax.numpy as jnp
from jax import lax

BLOCK = 896
SHELLS = 16
ANGLES = 64
ROWS = 14336
COLS = 14336
N_ROW = 16


class_count = 4


def shared_templates(key):
    radial = jax.random.normal(jax.random.fold_in(key, 1), (class_count, SHELLS, 2, 1), jnp.float32)
    angular = jax.random.normal(jax.random.fold_in(key, 2), (class_count, SHELLS, 2, ANGLES), jnp.float32)
    return (radial, angular)


def assemble(key, radial, angular, count, noise, falloff_base):
    labels = jax.random.randint(jax.random.fold_in(key, 3), (count,), 0, class_count)
    shifts = jax.random.randint(jax.random.fold_in(key, 4), (count,), 0, ANGLES)
    bins = jnp.arange(ANGLES, dtype=jnp.int32)
    index = (bins[None, :] - shifts[:, None]) % ANGLES
    picked = angular[labels]
    picked = jnp.take_along_axis(picked, jnp.broadcast_to(index[:, None, None, :], picked.shape), axis=3)
    falloff = falloff_base ** (-jnp.arange(SHELLS, dtype=jnp.float32) / (SHELLS - 1))
    value = falloff[None, :, None, None] * (0.7 * radial[labels] + 0.7 * picked) + 0.5 * noise
    return jnp.clip(value, -8.0, 8.0).reshape(count, SHELLS, 2 * ANGLES).astype(jnp.bfloat16)


def draw_row_coefs(key, part):
    radial, angular = shared_templates(key)
    key = jax.random.fold_in(key, 21)
    shape = (ROWS, SHELLS, 2, ANGLES)
    noise = jax.random.normal(jax.random.fold_in(key, 5), shape, jnp.float32)
    return assemble(key, radial, angular, ROWS, noise, 2.0)


def draw_col_coefs(key, part):
    radial, angular = shared_templates(key)
    key = jax.random.fold_in(key, 37)
    shape = (COLS, SHELLS, 2, ANGLES)
    noise = jax.random.normal(jax.random.fold_in(key, 5), shape, jnp.float32)
    return assemble(key, radial, angular, COLS, noise, 2.0)


def plant(array, key, low, top_value):
    extent = array.shape
    spot = [jax.random.randint(jax.random.fold_in(key, axis), (), 0, extent[axis]) for axis in range(len(extent))]
    array = array.at[tuple(spot)].set(low)
    longest = extent.index(max(extent))
    spot[longest] = (spot[longest] + 1) % extent[longest]
    return array.at[tuple(spot)].set(top_value)


def shard_levels(key, dims, shards, smallest, top_value):
    level = 1.0
    for position, parts in shards:
        heights = jax.random.uniform(jax.random.fold_in(jax.random.fold_in(key, 6), position), (parts,), jnp.float32, smallest / len(shards), top_value / len(shards))
        level = level * jnp.repeat(jnp.exp(heights), dims[position] // parts).reshape((-1,) + (1,) * (len(dims) - 1 - position))
    return level


def setup_inputs(seed: int = 0) -> dict:
    streams_of = jax.random.split(jax.random.key(seed), 7)
    return {
        "row_coefs": draw_row_coefs(jax.random.fold_in(streams_of[6], 71), 0),
        "col_coefs": draw_col_coefs(jax.random.fold_in(streams_of[6], 71), 0),
        "row_wedge": plant(jax.random.randint(streams_of[2], (ROWS,), 3, 9), jax.random.fold_in(streams_of[2], 1), 3, 8).astype(jnp.int32),
        "col_wedge": plant(jax.random.randint(streams_of[3], (COLS,), 3, 9), jax.random.fold_in(streams_of[3], 1), 3, 8).astype(jnp.int32),
        "rotation": jax.random.randint(streams_of[4], (1,), 0, ANGLES).astype(jnp.int32),
        "best_in": jnp.clip(-0.3 + 0.8 * jax.random.uniform(streams_of[5], (ROWS, COLS), jnp.float32) ** shard_levels(streams_of[5], (ROWS, COLS), ((0, 16), (1, 16)), -0.2, 0.2), -0.3, 0.5),
    }


def present(wedge, offset, angles):
    bins = jnp.arange(angles, dtype=jnp.int32)
    half = angles // 2
    phase = (bins[None, :] - offset - angles // 4) % half
    spread = jnp.minimum(phase, half - phase)
    return (spread > wedge[:, None]).astype(jnp.bfloat16)

def widened(mask):
    return jnp.concatenate([mask, mask], axis=-1)[:, None, :]

def turned(coefs, offset, angles):
    shape = coefs.shape
    split = coefs.reshape(shape[0], shape[1], 2, angles)
    return jnp.roll(split, offset, axis=3).reshape(shape)

def shell_energy(coefs, angles):
    squares = lax.optimization_barrier(jnp.sum(jnp.square(coefs.astype(jnp.float32)), axis=1))
    return squares[:, :angles] + squares[:, angles:]

def reference(row_coefs, col_coefs, row_wedge, col_wedge, rotation, best_in):
    offset = rotation[0].astype(jnp.int32)
    row_mask = present(row_wedge, jnp.int32(0), ANGLES)
    col_mask = present(col_wedge, offset, ANGLES)
    row_masked = row_coefs * widened(row_mask)
    col_masked = turned(col_coefs, offset, ANGLES) * widened(col_mask)
    row_energy = (shell_energy(row_masked, ANGLES) * 1.0).astype(jnp.bfloat16)
    col_energy = shell_energy(col_masked, ANGLES).astype(jnp.bfloat16)
    col_wide = col_masked.astype(jnp.float32)
    blocks_rows = row_masked.reshape(N_ROW, BLOCK, SHELLS, 2 * ANGLES)
    blocks_mask = row_mask.reshape(N_ROW, BLOCK, ANGLES)
    blocks_energy = row_energy.reshape(N_ROW, BLOCK, ANGLES)
    blocks_best = best_in.reshape(N_ROW, BLOCK, COLS)

    def one_block(inputs):
        rows_here, mask_here, energy_here, best_here = inputs
        cross = jnp.einsum('isk,jsk->ij', rows_here.astype(jnp.float32), col_wide)
        row_norm = jnp.dot(energy_here, col_mask.T, preferred_element_type=jnp.float32)
        col_norm = jnp.dot(mask_here, col_energy.T, preferred_element_type=jnp.float32)
        score = cross * lax.rsqrt(row_norm * col_norm + 1e-06)
        return jnp.maximum(best_here, score)
    result = lax.map(one_block, (blocks_rows, blocks_mask, blocks_energy, blocks_best))
    return result.reshape(ROWS, COLS)
```

```python
import functools

import jax
import jax.numpy as jnp
from jax import lax
from jax.experimental import pallas as pl
from jax.experimental.pallas import tpu as pltpu
from jax.sharding import PartitionSpec as P

BLOCK = 896
ANGLES = 64
HALF = 32
SHELLS = 16
NARROWEST = 3
BAND = 2 * NARROWEST + 1
AXES = ("row", "col")


def coordinates():
    return [(y, xl, c, z, xh) for y in range(4) for xl in range(2) for c in range(2) for z in range(8) for xh in range(2)]


def flat(y, xl, c, z, xh):
    return (y * 4 + xl * 2 + c) * 16 + z * 2 + xh


def shift(x, dy=0, dxl=0, dc=0, dz=0, dxh=0):
    pairs = [
        (flat(y, xl, c, z, xh), flat((y + dy) % 4, (xl + dxl) % 2, (c + dc) % 2, (z + dz) % 8, (xh + dxh) % 2))
        for y, xl, c, z, xh in coordinates()
    ]
    return lax.ppermute(x, AXES, pairs)


def kept_bin(k, turn):
    first = NARROWEST + 1
    low = jnp.maximum(turn - NARROWEST, first)
    skipped = jnp.maximum(turn + NARROWEST + 1 - low, 0)
    place = k + first
    return jnp.where(place < low, place, place + skipped)


def wedge_mask(bins, turn, wedge):
    phase = (bins - turn) & (HALF - 1)
    return jnp.minimum(phase, HALF - phase) > wedge


def prepare_kernel(n, rotation_ref, row_ref, col_ref, row_wedge_ref, col_wedge_ref, row_out, col_out):
    offset = rotation_ref[0] & (ANGLES - 1)
    turn = offset & (HALF - 1)
    rows = 4 * n

    def bins_of(shape):
        r = lax.broadcasted_iota(jnp.int32, shape, 0)
        part = jnp.where(r >= 2 * n, 1, 0)
        r = r - part * (2 * n)
        half = jnp.where(r >= n, 1, 0)
        return part, half, kept_bin(r - half * n, turn)

    part, half, bins = bins_of((rows, 2 * ANGLES))
    feature = lax.broadcasted_iota(jnp.int32, (rows, 2 * ANGLES), 1)
    angle = (bins + HALF * half + HALF // 2) & (ANGLES - 1)
    valid = bins < HALF - NARROWEST
    row_pick = jnp.where(valid & (feature == part * ANGLES + angle), 1.0, 0.0).astype(jnp.bfloat16)
    source = (angle - offset) & (ANGLES - 1)
    col_pick = jnp.where(valid & (feature == part * ANGLES + source), 1.0, 0.0).astype(jnp.bfloat16)
    _, _, bins = bins_of((rows, BLOCK))
    for pick, ref, wedge_ref, at, out in (
        (row_pick, row_ref, row_wedge_ref, 0, row_out),
        (col_pick, col_ref, col_wedge_ref, turn, col_out),
    ):
        picked = lax.dot_general(pick, ref[...], (((1,), (1,)), ((), ())), preferred_element_type=jnp.float32)
        mask = wedge_mask(bins, at, wedge_ref[...])
        out[0] = jnp.where(mask, picked, 0.0).astype(jnp.bfloat16)


def prepare(n, rotation, row_coefs, col_coefs, row_wedge, col_wedge):
    shape = jax.ShapeDtypeStruct((1, 4 * n, BLOCK), jnp.bfloat16)
    return pl.pallas_call(
        functools.partial(prepare_kernel, n),
        out_shape=[shape, shape],
        in_specs=[pl.BlockSpec(memory_space=pltpu.SMEM)] + [pl.BlockSpec(memory_space=pltpu.VMEM)] * 4,
        out_specs=[pl.BlockSpec(memory_space=pltpu.VMEM)] * 2,
        name="prepare",
    )(rotation, row_coefs.reshape(BLOCK, 2 * ANGLES), col_coefs.reshape(BLOCK, 2 * ANGLES), row_wedge.reshape(1, BLOCK), col_wedge.reshape(1, BLOCK))


def score_kernel(n, row_plan, col_plan, *refs):
    rotation_ref, row_wedge_ref, col_wedge_ref, best_ref = refs[:4]
    row_refs = refs[4 : 4 + len(row_plan)]
    col_refs = refs[4 + len(row_plan) : 4 + len(row_plan) + len(col_plan)]
    out_ref, left, right, best, result, best_sem, out_sem = refs[4 + len(row_plan) + len(col_plan) :]
    rows = 4 * n
    deep = left.shape[1]
    blocks = ((0, 512), (512, 384))
    loads = [
        pltpu.make_async_copy(best_ref.at[pl.ds(start, size)], best.at[pl.ds(start, size)], best_sem.at[i])
        for i, (start, size) in enumerate(blocks)
    ]
    for load in loads:
        load.start()
    turn = rotation_ref[0] & (HALF - 1)
    me_row, me_col = lax.axis_index("row"), lax.axis_index("col")
    y, xl, c = me_row >> 2, (me_row >> 1) & 1, me_row & 1
    z, xh = me_col >> 1, me_col & 1
    energies = []
    for wide, plan, pieces, place in (
        (left, row_plan, row_refs, lambda dz, dxh: ((z - dz) & 7) * 2 + (xh ^ dxh)),
        (right, col_plan, col_refs, lambda dy, dxl, dc: ((y - dy) & 3) * 4 + (xl ^ dxl) * 2 + (c ^ dc)),
    ):
        total = None
        for piece, shells in zip(pieces, plan):
            for i, shell in enumerate(shells):
                block = piece[i]
                at = place(*shell)
                if deep > rows:
                    wide[at, pl.ds(rows, deep - rows), :] = jnp.zeros((deep - rows, BLOCK), jnp.bfloat16)
                wide[at, pl.ds(0, rows), :] = block
                squares = jnp.square(block.astype(jnp.float32))
                total = squares if total is None else total + squares
        energies.append((total[: 2 * n] + total[2 * n :]).astype(jnp.bfloat16))
    row_energy, col_energy = energies
    r = lax.broadcasted_iota(jnp.int32, (2 * n, BLOCK), 0)
    bins = kept_bin(r - jnp.where(r >= n, n, 0), turn)
    row_mask = jnp.where(wedge_mask(bins, 0, row_wedge_ref[...]), 1.0, 0.0).astype(jnp.bfloat16)
    col_mask = jnp.where(wedge_mask(bins, turn, col_wedge_ref[...]), 1.0, 0.0).astype(jnp.bfloat16)

    def pairs(a, b):
        return lax.dot_general(a, b, (((0,), (0,)), ((), ())), preferred_element_type=jnp.float32)

    right_all = right[...].reshape(SHELLS * deep, BLOCK)
    stores = []
    for i, (start, size) in enumerate(blocks):
        cross = pairs(left[:, :, pl.ds(start, size)].reshape(SHELLS * deep, size), right_all)
        row_norm = pairs(row_energy[:, start : start + size], col_mask)
        col_norm = pairs(row_mask[:, start : start + size], col_energy)
        score = cross * lax.rsqrt(row_norm * col_norm + 1e-06)
        loads[i].wait()
        result[pl.ds(start, size), :] = jnp.maximum(best[pl.ds(start, size), :], score)
        store = pltpu.make_async_copy(result.at[pl.ds(start, size)], out_ref.at[pl.ds(start, size)], out_sem.at[i])
        store.start()
        stores.append(store)
    for store in stores:
        store.wait()


def scores(n, rotation, row_wedge, col_wedge, best_in, row_parts, col_parts):
    row_plan, col_plan = [p[1] for p in row_parts], [p[1] for p in col_parts]
    arrays = [p[0] for p in row_parts] + [p[0] for p in col_parts]
    deep = -(-4 * n // 16) * 16
    return pl.pallas_call(
        functools.partial(score_kernel, n, row_plan, col_plan),
        out_shape=jax.ShapeDtypeStruct((BLOCK, BLOCK), jnp.float32),
        in_specs=[pl.BlockSpec(memory_space=pltpu.SMEM)]
        + [pl.BlockSpec(memory_space=pltpu.VMEM)] * 2
        + [pl.BlockSpec(memory_space=pl.ANY)]
        + [pl.BlockSpec(memory_space=pltpu.VMEM)] * len(arrays),
        out_specs=pl.BlockSpec(memory_space=pl.ANY),
        scratch_shapes=[
            pltpu.VMEM((SHELLS, deep, BLOCK), jnp.bfloat16),
            pltpu.VMEM((SHELLS, deep, BLOCK), jnp.bfloat16),
            pltpu.VMEM((BLOCK, BLOCK), jnp.float32),
            pltpu.VMEM((BLOCK, BLOCK), jnp.float32),
            pltpu.SemaphoreType.DMA((2,)),
            pltpu.SemaphoreType.DMA((2,)),
        ],
        compiler_params=pltpu.CompilerParams(vmem_limit_bytes=40 * 1024 * 1024),
        cost_estimate=pl.CostEstimate(flops=2 * BLOCK * BLOCK * (SHELLS * deep + 4 * n), bytes_accessed=16 << 20, transcendentals=BLOCK * BLOCK),
        name="scores",
    )(rotation, row_wedge.reshape(1, BLOCK), col_wedge.reshape(1, BLOCK), best_in, *arrays)


def gather_rows(own):
    near = [shift(own, dz=1), shift(own, dz=-1)]
    mirror = shift(own, dxh=1)
    far = [shift(own, dz=2), shift(own, dz=-2)]
    opposite = shift(own, dz=4)
    farther = [shift(far[0], dz=1), shift(far[1], dz=-1)]
    groups = [
        (jnp.concatenate(near), [(1, 0), (-1, 0)]),
        (jnp.concatenate(far + [opposite]), [(2, 0), (-2, 0), (4, 0)]),
        (jnp.concatenate(farther), [(3, 0), (-3, 0)]),
    ]
    parts = [(own, [(0, 0)]), (mirror, [(0, 1)])]
    for array, shells in groups:
        parts.append((array, shells))
        parts.append((shift(array, dxh=1), [(dz, 1) for dz, _ in shells]))
    return parts


def gather_cols(own):
    pair = jnp.concatenate([own, shift(own, dxl=1)])
    around = [pair, shift(pair, dy=1), shift(pair, dy=-1), shift(pair, dy=2)]
    shells = [(dy, dxl, 0) for dy in (0, 1, -1, 2) for dxl in (0, 1)]
    chip = jnp.concatenate(around)
    return [(chip, shells), (shift(chip, dc=1), [(dy, dxl, 1) for dy, dxl, _ in shells])]


def with_bins(n, row_coefs, col_coefs, row_wedge, col_wedge, rotation, best_in):
    row_own, col_own = prepare(n, rotation, row_coefs, col_coefs, row_wedge, col_wedge)
    row_parts = gather_rows(row_own)
    col_parts = gather_cols(col_own)
    return scores(n, rotation, row_wedge, col_wedge, best_in, row_parts, col_parts)


def shards(row_coefs, col_coefs, row_wedge, col_wedge, rotation, best_in):
    turn = rotation[0] & (HALF - 1)
    apart = jnp.minimum(jnp.minimum(turn, HALF - turn), BAND)
    branches = [functools.partial(with_bins, n) for n in (18, 20, 22, 24, 26)]
    return lax.switch((BAND + 1 - apart) // 2, branches, row_coefs, col_coefs, row_wedge, col_wedge, rotation, best_in)


def solution(mesh):
    return jax.shard_map(
        shards,
        mesh=mesh,
        in_specs=(
            P("row", "col", None),
            P("col", "row", None),
            P("row"),
            P("col"),
            P(),
            P("row", "col"),
        ),
        out_specs=P("row", "col"),
        check_vma=False,
    )
```

```python
import functools

import jax
import jax.numpy as jnp
from jax import lax
from jax.experimental import pallas as pl
from jax.experimental.pallas import tpu as pltpu
from jax.sharding import PartitionSpec as P

BLOCK = 896
ANGLES = 64
HALF = 32
SHELLS = 16
NARROWEST = 3
LANES = 128
BAND = 2 * NARROWEST + 1
AXES = ("row", "col")


def coordinates():
    return [(y, xl, c, z, xh) for y in range(4) for xl in range(2) for c in range(2) for z in range(8) for xh in range(2)]


def flat(y, xl, c, z, xh):
    return (y * 4 + xl * 2 + c) * 16 + z * 2 + xh


def shift(x, dy=0, dxl=0, dc=0, dz=0, dxh=0):
    pairs = [
        (flat(y, xl, c, z, xh), flat((y + dy) % 4, (xl + dxl) % 2, (c + dc) % 2, (z + dz) % 8, (xh + dxh) % 2))
        for y, xl, c, z, xh in coordinates()
    ]
    return lax.ppermute(x, AXES, pairs)


def kept_bin(k, turn):
    first = NARROWEST + 1
    low = jnp.maximum(turn - NARROWEST, first)
    skipped = jnp.maximum(turn + NARROWEST + 1 - low, 0)
    place = k + first
    return jnp.where(place < low, place, place + skipped)


def wedge_mask(bins, turn, wedge):
    phase = (bins - turn) & (HALF - 1)
    return jnp.minimum(phase, HALF - phase) > wedge


def prepare_kernel(n, rotation_ref, row_ref, col_ref, row_wedge_ref, col_wedge_ref, row_out, col_out):
    offset = rotation_ref[0] & (ANGLES - 1)
    turn = offset & (HALF - 1)
    rows = 4 * n

    def bins_of(shape):
        r = lax.broadcasted_iota(jnp.int32, shape, 0)
        part = jnp.where(r >= 2 * n, 1, 0)
        r = r - part * (2 * n)
        half = jnp.where(r >= n, 1, 0)
        return part, half, kept_bin(r - half * n, turn)

    part, half, bins = bins_of((rows, 2 * ANGLES))
    feature = lax.broadcasted_iota(jnp.int32, (rows, 2 * ANGLES), 1)
    angle = (bins + HALF * half + HALF // 2) & (ANGLES - 1)
    valid = bins < HALF - NARROWEST
    row_pick = jnp.where(valid & (feature == part * ANGLES + angle), 1.0, 0.0).astype(jnp.bfloat16)
    source = (angle - offset) & (ANGLES - 1)
    col_pick = jnp.where(valid & (feature == part * ANGLES + source), 1.0, 0.0).astype(jnp.bfloat16)
    _, _, bins = bins_of((rows, LANES))

    def block(j, carry):
        at = pl.ds(pl.multiple_of(j * LANES, LANES), LANES)
        for pick, ref, wedge_ref, centre, out in (
            (row_pick, row_ref, row_wedge_ref, 0, row_out),
            (col_pick, col_ref, col_wedge_ref, turn, col_out),
        ):
            picked = lax.dot_general(pick, ref[at, :], (((1,), (1,)), ((), ())), preferred_element_type=jnp.float32)
            mask = wedge_mask(bins, centre, wedge_ref[:, at])
            out[0, :, at] = jnp.where(mask, picked, 0.0).astype(jnp.bfloat16)
        return carry

    lax.fori_loop(0, BLOCK // LANES, block, 0)


def prepare(n, rotation, row_coefs, col_coefs, row_wedge, col_wedge):
    shape = jax.ShapeDtypeStruct((1, 4 * n, BLOCK), jnp.bfloat16)
    return pl.pallas_call(
        functools.partial(prepare_kernel, n),
        out_shape=[shape, shape],
        in_specs=[pl.BlockSpec(memory_space=pltpu.SMEM)] + [pl.BlockSpec(memory_space=pltpu.VMEM)] * 4,
        out_specs=[pl.BlockSpec(memory_space=pltpu.VMEM)] * 2,
        name="prepare",
    )(rotation, row_coefs.reshape(BLOCK, 2 * ANGLES), col_coefs.reshape(BLOCK, 2 * ANGLES), row_wedge, col_wedge)


STRIPE = 224
STRIPES = BLOCK // STRIPE


def score_kernel(n, row_plan, col_plan, *refs):
    rotation_ref, row_wedge_ref, col_wedge_ref, best_ref = refs[:4]
    row_refs = refs[4 : 4 + len(row_plan)]
    col_refs = refs[4 + len(row_plan) : 4 + len(row_plan) + len(col_plan)]
    out_ref, column, left, right, side, col_masks, col_energies, best, result, best_sem, out_sem = refs[4 + len(row_plan) + len(col_plan) :]
    rows = 4 * n
    deep = right.shape[1]
    half = side.shape[1] // 2

    def fetch(m):
        at = pl.ds(m * STRIPE, STRIPE)
        return pltpu.make_async_copy(best_ref.at[at], best.at[at], best_sem.at[m])

    def store(m):
        at = pl.ds(m * STRIPE, STRIPE)
        return pltpu.make_async_copy(result.at[at], out_ref.at[at], out_sem.at[m])

    for m in range(STRIPES):
        fetch(m).start()
    turn = rotation_ref[0] & (HALF - 1)
    me_row, me_col = lax.axis_index("row"), lax.axis_index("col")
    y, xl, c = me_row >> 2, (me_row >> 1) & 1, me_row & 1
    z, xh = me_col >> 1, me_col & 1
    r = lax.broadcasted_iota(jnp.int32, (half, LANES), 0)
    bins = kept_bin(r - jnp.where(r >= n, n, 0), turn)
    counted = r < 2 * n

    def gathered(pieces, plan, place, wide, at, to):
        total = None
        for piece, shells in zip(pieces, plan):
            for i, shell in enumerate(shells):
                block = piece[i, :, at]
                slot = place(*shell)
                wide[slot, pl.ds(0, rows), to] = block
                if deep > rows:
                    wide[slot, pl.ds(rows, deep - rows), to] = jnp.zeros((deep - rows, LANES), jnp.bfloat16)
                squares = jnp.square(block.astype(jnp.float32))
                total = squares if total is None else total + squares
        energy = (total[: 2 * n] + total[2 * n :]).astype(jnp.bfloat16)
        return jnp.concatenate([energy, jnp.zeros((half - 2 * n, LANES), jnp.bfloat16)])

    def row_slot(dz, dxh):
        return (dz & 7) * 2 + dxh

    def col_slot(dy, dxl, dc):
        shell = ((y - dy) & 3) * 4 + (xl ^ dxl) * 2 + (c ^ dc)
        return ((z - (shell >> 1)) & 7) * 2 + (xh ^ (shell & 1))

    def masks(centre, wedge):
        return jnp.where(counted & wedge_mask(bins, centre, wedge), 1.0, 0.0).astype(jnp.bfloat16)

    nothing = jnp.zeros((half, LANES), jnp.bfloat16)

    def assemble(j, carry):
        at = pl.ds(pl.multiple_of(j * LANES, LANES), LANES)
        energy = gathered(row_refs, row_plan, row_slot, column, at, pl.ds(0, LANES))
        left[at, :] = column[...].reshape(SHELLS * deep, LANES).T
        side[at, :] = jnp.concatenate([energy, masks(0, row_wedge_ref[:, at])]).T
        energy = gathered(col_refs, col_plan, col_slot, right, at, at)
        col_masks[:, at] = jnp.concatenate([masks(turn, col_wedge_ref[:, at]), nothing])
        col_energies[:, at] = jnp.concatenate([nothing, energy])
        return carry

    lax.fori_loop(0, BLOCK // LANES, assemble, 0)

    def product(a, b):
        return jnp.dot(a, b, preferred_element_type=jnp.float32)

    def stripe(m, carry):
        at = pl.ds(pl.multiple_of(m * STRIPE, STRIPE), STRIPE)
        cross = product(left[at, :], right[...].reshape(SHELLS * deep, BLOCK))
        row_norm = product(side[at, :], col_masks[...])
        col_norm = product(side[at, :], col_energies[...])
        score = cross * lax.rsqrt(row_norm * col_norm + 1e-06)
        fetch(m).wait()
        result[at, :] = jnp.maximum(best[at, :], score)
        store(m).start()
        return carry

    lax.fori_loop(0, STRIPES, stripe, 0)
    for m in range(STRIPES):
        store(m).wait()


def scores(n, rotation, row_wedge, col_wedge, best_in, row_parts, col_parts):
    row_plan, col_plan = [p[1] for p in row_parts], [p[1] for p in col_parts]
    arrays = [p[0] for p in row_parts] + [p[0] for p in col_parts]
    deep = -(-4 * n // 16) * 16
    return pl.pallas_call(
        functools.partial(score_kernel, n, row_plan, col_plan),
        out_shape=jax.ShapeDtypeStruct((BLOCK, BLOCK), jnp.float32),
        in_specs=[pl.BlockSpec(memory_space=pltpu.SMEM)]
        + [pl.BlockSpec(memory_space=pltpu.VMEM)] * 2
        + [pl.BlockSpec(memory_space=pltpu.HBM)]
        + [pl.BlockSpec(memory_space=pltpu.VMEM)] * len(arrays),
        out_specs=pl.BlockSpec(memory_space=pltpu.HBM),
        scratch_shapes=[
            pltpu.VMEM((SHELLS, deep, LANES), jnp.bfloat16),
            pltpu.VMEM((BLOCK, SHELLS * deep), jnp.bfloat16),
            pltpu.VMEM((SHELLS, deep, BLOCK), jnp.bfloat16),
            pltpu.VMEM((BLOCK, LANES), jnp.bfloat16),
            pltpu.VMEM((LANES, BLOCK), jnp.bfloat16),
            pltpu.VMEM((LANES, BLOCK), jnp.bfloat16),
            pltpu.VMEM((BLOCK, BLOCK), jnp.float32),
            pltpu.VMEM((BLOCK, BLOCK), jnp.float32),
            pltpu.SemaphoreType.DMA((STRIPES,)),
            pltpu.SemaphoreType.DMA((STRIPES,)),
        ],
        compiler_params=pltpu.CompilerParams(vmem_limit_bytes=40 * 1024 * 1024),
        cost_estimate=pl.CostEstimate(flops=2 * BLOCK * BLOCK * (SHELLS * deep + 4 * n), bytes_accessed=16 << 20, transcendentals=BLOCK * BLOCK),
        name="scores",
    )(rotation, row_wedge, col_wedge, best_in, *arrays)


def gather(row_own, col_own):
    together = lax.optimization_barrier
    row_pair = jnp.concatenate([row_own, shift(row_own, dxh=1)])
    col_pair = jnp.concatenate([col_own, shift(col_own, dxl=1)])
    row_pair, col_pair = together((row_pair, col_pair))
    rows = [(row_pair, [(0, 0), (0, 1)])]
    up, down = shift(row_pair, dz=1), shift(row_pair, dz=-1)
    chip = jnp.concatenate([col_pair, shift(col_pair, dy=1), shift(col_pair, dy=-1), shift(col_pair, dy=2)])
    places = [(dy, dxl) for dy in (0, 1, -1, 2) for dxl in (0, 1)]
    up, down = together((up, down))
    rows += [(up, [(1, 0), (1, 1)]), (down, [(-1, 0), (-1, 1)])]
    up, down = shift(up, dz=1), shift(down, dz=-1)
    up, down, chip = together((up, down, chip))
    rows += [(up, [(2, 0), (2, 1)]), (down, [(-2, 0), (-2, 1)])]
    up, down = shift(up, dz=1), shift(down, dz=-1)
    other = shift(chip, dc=1)
    up, down, other = together((up, down, other))
    rows += [(up, [(3, 0), (3, 1)]), (down, [(-3, 0), (-3, 1)])]
    rows += [(shift(up[:1], dz=1), [(4, 0)]), (shift(down[1:], dz=-1), [(4, 1)])]
    cols = [(chip, [(dy, dxl, 0) for dy, dxl in places]), (other, [(dy, dxl, 1) for dy, dxl in places])]
    return rows, cols


def with_bins(n, row_coefs, col_coefs, row_wedge, col_wedge, rotation, best_in):
    row_wedge, col_wedge = row_wedge.reshape(1, BLOCK), col_wedge.reshape(1, BLOCK)
    row_parts, col_parts = gather(*prepare(n, rotation, row_coefs, col_coefs, row_wedge, col_wedge))
    return scores(n, rotation, row_wedge, col_wedge, best_in, row_parts, col_parts)


def shards(row_coefs, col_coefs, row_wedge, col_wedge, rotation, best_in):
    turn = rotation[0] & (HALF - 1)
    apart = jnp.minimum(jnp.minimum(turn, HALF - turn), BAND)
    branches = [functools.partial(with_bins, n) for n in (18, 20, 22, 24, 26)]
    return lax.cond(apart < BAND, functools.partial(with_bins, 26), functools.partial(with_bins, 18), row_coefs, col_coefs, row_wedge, col_wedge, rotation, best_in)


def solution(mesh):
    return jax.shard_map(
        shards,
        mesh=mesh,
        in_specs=(
            P("row", "col", None),
            P("col", "row", None),
            P("row"),
            P("col"),
            P(),
            P("row", "col"),
        ),
        out_specs=P("row", "col"),
        check_vma=False,
    )
```

```python
import functools

import jax
import jax.numpy as jnp
from jax import lax
from jax.experimental import pallas as pl
from jax.experimental.pallas import tpu as pltpu
from jax.sharding import PartitionSpec as P

BLOCK = 896
ANGLES = 64
HALF = 32
SHELLS = 16
NARROWEST = 3
LANES = 128
BAND = 2 * NARROWEST + 1
AXES = ("row", "col")


def coordinates():
    return [(y, xl, c, z, xh) for y in range(4) for xl in range(2) for c in range(2) for z in range(8) for xh in range(2)]


def flat(y, xl, c, z, xh):
    return (y * 4 + xl * 2 + c) * 16 + z * 2 + xh


def shift(x, dy=0, dxl=0, dc=0, dz=0, dxh=0):
    pairs = [
        (flat(y, xl, c, z, xh), flat((y + dy) % 4, (xl + dxl) % 2, (c + dc) % 2, (z + dz) % 8, (xh + dxh) % 2))
        for y, xl, c, z, xh in coordinates()
    ]
    return lax.ppermute(x, AXES, pairs)


def kept_bin(k, turn):
    first = NARROWEST + 1
    low = jnp.maximum(turn - NARROWEST, first)
    skipped = jnp.maximum(turn + NARROWEST + 1 - low, 0)
    place = k + first
    return jnp.where(place < low, place, place + skipped)


def wedge_mask(bins, turn, wedge):
    phase = (bins - turn) & (HALF - 1)
    return jnp.minimum(phase, HALF - phase) > wedge


def prepare_kernel(n, rotation_ref, row_ref, col_ref, row_wedge_ref, col_wedge_ref, row_out, col_out, rotation, row_coefs, col_coefs, row_wedge, col_wedge, sems):
    pairs = (
        (rotation_ref, rotation),
        (row_wedge_ref, row_wedge),
        (row_ref, row_coefs),
        (col_wedge_ref, col_wedge),
        (col_ref, col_coefs),
    )
    loads = [pltpu.make_async_copy(source, target, sems.at[i]) for i, (source, target) in enumerate(pairs)]
    for load in loads:
        load.start()
    loads[0].wait()
    offset = rotation[0] & (ANGLES - 1)
    turn = offset & (HALF - 1)
    rows = 4 * n

    def bins_of(shape):
        r = lax.broadcasted_iota(jnp.int32, shape, 0)
        part = jnp.where(r >= 2 * n, 1, 0)
        r = r - part * (2 * n)
        half = jnp.where(r >= n, 1, 0)
        return part, half, kept_bin(r - half * n, turn)

    part, half, bins = bins_of((rows, 2 * ANGLES))
    feature = lax.broadcasted_iota(jnp.int32, (rows, 2 * ANGLES), 1)
    angle = (bins + HALF * half + HALF // 2) & (ANGLES - 1)
    valid = bins < HALF - NARROWEST
    row_pick = jnp.where(valid & (feature == part * ANGLES + angle), 1.0, 0.0).astype(jnp.bfloat16)
    source = (angle - offset) & (ANGLES - 1)
    col_pick = jnp.where(valid & (feature == part * ANGLES + source), 1.0, 0.0).astype(jnp.bfloat16)
    _, _, bins = bins_of((rows, 1))
    for ready, pick, coefs, wedge, centre, out in (
        (loads[1:3], row_pick, row_coefs, row_wedge, 0, row_out),
        (loads[3:], col_pick, col_coefs, col_wedge, turn, col_out),
    ):
        for load in ready:
            load.wait()
        phase = (bins - centre) & (HALF - 1)
        spread = jnp.minimum(phase, HALF - phase)
        mask = spread > wedge[...].reshape(1, BLOCK)
        picked = lax.dot_general(pick, coefs[...], (((1,), (1,)), ((), ())), preferred_element_type=jnp.float32)
        out[0] = jnp.where(mask, picked, 0.0).astype(jnp.bfloat16)


def prepare(n, rotation, row_coefs, col_coefs, row_wedge, col_wedge):
    shape = jax.ShapeDtypeStruct((1, 4 * n, BLOCK), jnp.bfloat16)
    return pl.pallas_call(
        functools.partial(prepare_kernel, n),
        out_shape=[shape, shape],
        in_specs=[pl.BlockSpec(memory_space=pltpu.HBM)] * 5,
        out_specs=[pl.BlockSpec(memory_space=pltpu.VMEM)] * 2,
        scratch_shapes=[pltpu.SMEM((1,), jnp.int32)]
        + [pltpu.VMEM((BLOCK, 2 * ANGLES), jnp.bfloat16)] * 2
        + [pltpu.VMEM((BLOCK,), jnp.int32)] * 2
        + [pltpu.SemaphoreType.DMA((5,))],
        compiler_params=pltpu.CompilerParams(vmem_limit_bytes=8 * 1024 * 1024),
        name="prepare",
    )(rotation, row_coefs.reshape(BLOCK, 2 * ANGLES), col_coefs.reshape(BLOCK, 2 * ANGLES), row_wedge, col_wedge)


STRIPE = 448
FINISH_LIMIT = 16
STRIPES = BLOCK // STRIPE
SIDE = 64


def lanes(j):
    return pl.ds(pl.multiple_of(j * LANES, LANES), LANES)


def wedge_masks(n, rotation_ref, centre, wedge):
    turn = rotation_ref[0] & (HALF - 1)
    r = lax.broadcasted_iota(jnp.int32, (SIDE, LANES), 0)
    bins = kept_bin(r - jnp.where(r >= n, n, 0), turn)
    return jnp.where((r < 2 * n) & wedge_mask(bins, centre, wedge), 1.0, 0.0).astype(jnp.bfloat16)


def energy(n, total):
    both = (total[: 2 * n] + total[2 * n :]).astype(jnp.bfloat16)
    return jnp.concatenate([both, jnp.zeros((SIDE - 2 * n, LANES), jnp.bfloat16)])


def place(wide, slot, block, to):
    rows, deep = block.shape[0], wide.shape[1]
    wide[slot, pl.ds(0, rows), to] = block
    if deep > rows:
        wide[slot, pl.ds(rows, deep - rows), to] = jnp.zeros((deep - rows, LANES), jnp.bfloat16)


def product(a, b):
    return jnp.dot(a, b, preferred_element_type=jnp.float32)


def row_slot(dz, dxh):
    d = dz & 7
    return jnp.where(d == 0, 0, jnp.where(d <= 4, 2 * d - 1, 2 * (8 - d))) * 2 + dxh


def col_slot(dy, dxl, dc):
    me_row, me_col = lax.axis_index("row"), lax.axis_index("col")
    y, xl, c = me_row >> 2, (me_row >> 1) & 1, me_row & 1
    z, xh = me_col >> 1, me_col & 1
    shell = ((y - dy) & 3) * 4 + (xl ^ dxl) * 2 + (c ^ dc)
    return row_slot(z - (shell >> 1), xh ^ (shell & 1))


def gathered(pieces, total, wide, slots, at, to):
    shells = [piece[i, :, at] for piece in pieces for i in range(piece.shape[0])]
    for slot, block in zip(slots, shells):
        place(wide, slot, block, to)
        squares = jnp.square(block.astype(jnp.float32))
        total = squares if total is None else total + squares
    return total


def turned_rows(left, column, at, start):
    wide = column.shape[0] * column.shape[1]
    left[at, pl.ds(start, wide)] = column[...].reshape(wide, LANES).T


def begin_kernel(places, *refs):
    rows, chip = refs[:4], refs[4]
    left, right, row_sums, col_sums, column = refs[5:]
    slots = [col_slot(dy, dxl, 0) for dy, dxl in places]

    def assemble(j, carry):
        at = lanes(j)
        row_sums[:, at] = gathered(rows, None, column, range(8), at, pl.ds(0, LANES))
        turned_rows(left, column, at, 0)
        col_sums[:, at] = gathered([chip], None, right, slots, at, at)
        return carry

    lax.fori_loop(0, BLOCK // LANES, assemble, 0)


def partial_kernel(n, places, rotation_ref, col_wedge_ref, down2, up3, down3, other, early_row_sums, early_col_sums, _, __, left, right, cross_ref, sums_ref, col_masks, col_energies, column):
    deep = right.shape[1]
    start = 8 * deep
    slots = [col_slot(dy, dxl, 1) for dy, dxl in places]
    turn = rotation_ref[0] & (HALF - 1)
    nothing = jnp.zeros((SIDE, LANES), jnp.bfloat16)

    def assemble(j, carry):
        at = lanes(j)
        sums_ref[:, at] = gathered([down2, up3, down3], early_row_sums[:, at], column, range(6), at, pl.ds(0, LANES))
        turned_rows(left, column, at, start)
        total = gathered([other], early_col_sums[:, at], right, slots, at, at)
        col_masks[:, at] = jnp.concatenate([wedge_masks(n, rotation_ref, turn, col_wedge_ref[:, at]), nothing])
        col_energies[:, at] = jnp.concatenate([nothing, energy(n, total)])
        return carry

    lax.fori_loop(0, BLOCK // LANES, assemble, 0)

    def stripe(m, carry):
        at = pl.ds(pl.multiple_of(m * STRIPE, STRIPE), STRIPE)
        cross_ref[at, :] = product(left[at, :], right[: SHELLS - 2].reshape((SHELLS - 2) * deep, BLOCK))
        return carry

    lax.fori_loop(0, STRIPES, stripe, 0, unroll=True)


def finish_kernel(n, rotation_ref, row_wedge_ref, best_ref, cross_ref, sums_ref, right, col_masks, col_energies, first, second, out_ref, column, left, side):
    late = left.shape[1]

    def assemble(j, carry):
        at = lanes(j)
        total = gathered([first, second], sums_ref[:, at], column, range(2), at, pl.ds(0, LANES))
        turned_rows(left, column, at, 0)
        side[at, :] = jnp.concatenate([energy(n, total), wedge_masks(n, rotation_ref, 0, row_wedge_ref[:, at])]).T
        return carry

    lax.fori_loop(0, BLOCK // LANES, assemble, 0)

    def stripe(m, carry):
        at = pl.ds(pl.multiple_of(m * STRIPE, STRIPE), STRIPE)
        cross = cross_ref[at, :] + product(left[at, :], right[SHELLS - 2 :].reshape(late, BLOCK))
        row_norm = product(side[at, :], col_masks[...])
        col_norm = product(side[at, :], col_energies[...])
        score = cross * lax.rsqrt(row_norm * col_norm + 1e-06)
        out_ref[at, :] = jnp.maximum(best_ref[at, :], score)
        return carry

    lax.fori_loop(0, STRIPES, stripe, 0, unroll=True)


SMEM, VMEM = pl.BlockSpec(memory_space=pltpu.SMEM), pl.BlockSpec(memory_space=pltpu.VMEM)
MIB = 1024 * 1024


def begin(n, rows, chip, places):
    deep = -(-4 * n // 16) * 16
    sums = jax.ShapeDtypeStruct((4 * n, BLOCK), jnp.float32)
    return pl.pallas_call(
        functools.partial(begin_kernel, places),
        out_shape=[
            jax.ShapeDtypeStruct((BLOCK, (SHELLS - 2) * deep), jnp.bfloat16),
            jax.ShapeDtypeStruct((SHELLS, deep, BLOCK), jnp.bfloat16),
            sums,
            sums,
        ],
        in_specs=[VMEM] * 5,
        out_specs=[VMEM] * 4,
        scratch_shapes=[pltpu.VMEM((8, deep, LANES), jnp.bfloat16)],
        compiler_params=pltpu.CompilerParams(vmem_limit_bytes=8 * MIB),
        cost_estimate=pl.CostEstimate(flops=16 * 8 * n * BLOCK, bytes_accessed=6 * MIB, transcendentals=0),
        name="begin",
    )(*rows, chip)


def partial_cross(n, rotation, col_wedge, late, other, begun, places):
    left, right, row_sums, col_sums = begun
    deep = right.shape[1]
    sides = jax.ShapeDtypeStruct((2 * SIDE, BLOCK), jnp.bfloat16)
    return pl.pallas_call(
        functools.partial(partial_kernel, n, places),
        out_shape=[
            jax.ShapeDtypeStruct(left.shape, left.dtype),
            jax.ShapeDtypeStruct(right.shape, right.dtype),
            jax.ShapeDtypeStruct((BLOCK, BLOCK), jnp.float32),
            jax.ShapeDtypeStruct((4 * n, BLOCK), jnp.float32),
            sides,
            sides,
        ],
        in_specs=[SMEM] + [VMEM] * 9,
        out_specs=[VMEM] * 6,
        scratch_shapes=[pltpu.VMEM((6, deep, LANES), jnp.bfloat16)],
        input_output_aliases={8: 0, 9: 1},
        compiler_params=pltpu.CompilerParams(vmem_limit_bytes=16 * MIB),
        cost_estimate=pl.CostEstimate(flops=2 * BLOCK * BLOCK * (SHELLS - 2) * deep, bytes_accessed=8 * MIB, transcendentals=0),
        name="partial_cross",
    )(rotation, col_wedge, *late, other, row_sums, col_sums, left, right)


def finish(n, rotation, row_wedge, best_in, cross, sums, right, col_masks, col_energies, last):
    deep = right.shape[1]
    return pl.pallas_call(
        functools.partial(finish_kernel, n),
        out_shape=jax.ShapeDtypeStruct((BLOCK, BLOCK), jnp.float32),
        in_specs=[SMEM] + [VMEM] * 9,
        out_specs=VMEM,
        scratch_shapes=[
            pltpu.VMEM((2, deep, LANES), jnp.bfloat16),
            pltpu.VMEM((BLOCK, 2 * deep), jnp.bfloat16),
            pltpu.VMEM((BLOCK, LANES), jnp.bfloat16),
        ],
        compiler_params=pltpu.CompilerParams(vmem_limit_bytes=FINISH_LIMIT * MIB),
        cost_estimate=pl.CostEstimate(flops=2 * BLOCK * BLOCK * (2 * deep + 4 * SIDE), bytes_accessed=8 * MIB, transcendentals=BLOCK * BLOCK),
        name="finish",
    )(rotation, row_wedge, best_in, cross, sums, right, col_masks, col_energies, *last)


def with_bins(n, row_coefs, col_coefs, row_wedge, col_wedge, rotation, best_in):
    row_own, col_own = prepare(n, rotation, row_coefs, col_coefs, row_wedge, col_wedge)
    row_wedge, col_wedge = row_wedge.reshape(1, BLOCK), col_wedge.reshape(1, BLOCK)
    together = lax.optimization_barrier
    pair = jnp.concatenate([row_own, shift(row_own, dxh=1)])
    col_pair = jnp.concatenate([col_own, shift(col_own, dxl=1)])
    pair, col_pair = together((pair, col_pair))
    up1, down1 = shift(pair, dz=1), shift(pair, dz=-1)
    chip = jnp.concatenate([col_pair, shift(col_pair, dy=1), shift(col_pair, dy=-1), shift(col_pair, dy=2)])
    places = [(dy, dxl) for dy in (0, 1, -1, 2) for dxl in (0, 1)]
    up1, down1 = together((up1, down1))
    up2, down2 = shift(up1, dz=1), shift(down1, dz=-1)
    up2, down2, chip = together((up2, down2, chip))
    up3, down3 = shift(up2, dz=1), shift(down2, dz=-1)
    begun = begin(n, (pair, up1, down1, up2), chip, places)
    up3, down3, chip, begun = together((up3, down3, chip, begun))
    other = shift(chip, dc=1)
    last = (shift(up3[:1], dz=1), shift(down3[1:], dz=-1))
    _, right, cross, sums, masks, energies = partial_cross(n, rotation, col_wedge, (down2, up3, down3), other, begun, places)
    return finish(n, rotation, row_wedge, best_in, cross, sums, right, masks, energies, last)


def shards(row_coefs, col_coefs, row_wedge, col_wedge, rotation, best_in):
    turn = rotation[0] & (HALF - 1)
    apart = jnp.minimum(jnp.minimum(turn, HALF - turn), BAND)
    branches = [functools.partial(with_bins, n) for n in (18, 20, 22, 24, 26)]
    return lax.cond(apart < BAND, functools.partial(with_bins, 26), functools.partial(with_bins, 18), row_coefs, col_coefs, row_wedge, col_wedge, rotation, best_in)


def solution(mesh):
    return jax.shard_map(
        shards,
        mesh=mesh,
        in_specs=(
            P("row", "col", None),
            P("col", "row", None),
            P("row"),
            P("col"),
            P(),
            P("row", "col"),
        ),
        out_specs=P("row", "col"),
        check_vma=False,
    )
```

```python
import functools

import jax
import jax.numpy as jnp
from jax import lax
from jax.experimental import pallas as pl
from jax.experimental.pallas import tpu as pltpu
from jax.sharding import PartitionSpec as P

BLOCK = 896
ANGLES = 64
HALF = 32
SHELLS = 16
NARROWEST = 3
LANES = 128
BAND = 2 * NARROWEST + 1
AXES = ("row", "col")


def coordinates():
    return [(y, xl, c, z, xh) for y in range(4) for xl in range(2) for c in range(2) for z in range(8) for xh in range(2)]


def flat(y, xl, c, z, xh):
    return (y * 4 + xl * 2 + c) * 16 + z * 2 + xh


def shift(x, dy=0, dxl=0, dc=0, dz=0, dxh=0):
    pairs = [
        (flat(y, xl, c, z, xh), flat((y + dy) % 4, (xl + dxl) % 2, (c + dc) % 2, (z + dz) % 8, (xh + dxh) % 2))
        for y, xl, c, z, xh in coordinates()
    ]
    return lax.ppermute(x, AXES, pairs)


def kept_bin(k, turn):
    first = NARROWEST + 1
    low = jnp.maximum(turn - NARROWEST, first)
    skipped = jnp.maximum(turn + NARROWEST + 1 - low, 0)
    place = k + first
    return jnp.where(place < low, place, place + skipped)


def wedge_mask(bins, turn, wedge):
    phase = (bins - turn) & (HALF - 1)
    return jnp.minimum(phase, HALF - phase) > wedge


def prepare_kernel(n, rotation_ref, row_ref, col_ref, row_wedge_ref, col_wedge_ref, row_out, col_out, rotation, row_coefs, col_coefs, row_wedge, col_wedge, sems):
    pairs = (
        (rotation_ref, rotation),
        (row_wedge_ref, row_wedge),
        (row_ref, row_coefs),
        (col_wedge_ref, col_wedge),
        (col_ref, col_coefs),
    )
    loads = [pltpu.make_async_copy(source, target, sems.at[i]) for i, (source, target) in enumerate(pairs)]
    for load in loads:
        load.start()
    loads[0].wait()
    offset = rotation[0] & (ANGLES - 1)
    turn = offset & (HALF - 1)
    rows = 4 * n

    def bins_of(shape):
        r = lax.broadcasted_iota(jnp.int32, shape, 0)
        part = jnp.where(r >= 2 * n, 1, 0)
        r = r - part * (2 * n)
        half = jnp.where(r >= n, 1, 0)
        return part, half, kept_bin(r - half * n, turn)

    part, half, bins = bins_of((rows, 2 * ANGLES))
    feature = lax.broadcasted_iota(jnp.int32, (rows, 2 * ANGLES), 1)
    angle = (bins + HALF * half + HALF // 2) & (ANGLES - 1)
    valid = bins < HALF - NARROWEST
    row_pick = jnp.where(valid & (feature == part * ANGLES + angle), 1.0, 0.0).astype(jnp.bfloat16)
    source = (angle - offset) & (ANGLES - 1)
    col_pick = jnp.where(valid & (feature == part * ANGLES + source), 1.0, 0.0).astype(jnp.bfloat16)
    _, _, bins = bins_of((rows, 1))
    for ready, pick, coefs, wedge, centre, out in (
        (loads[1:3], row_pick, row_coefs, row_wedge, 0, row_out),
        (loads[3:], col_pick, col_coefs, col_wedge, turn, col_out),
    ):
        for load in ready:
            load.wait()
        phase = (bins - centre) & (HALF - 1)
        spread = jnp.minimum(phase, HALF - phase)
        mask = spread > wedge[...].reshape(1, BLOCK)
        picked = lax.dot_general(pick, coefs[...], (((1,), (1,)), ((), ())), preferred_element_type=jnp.float32)
        out[0] = jnp.where(mask, picked, 0.0).astype(jnp.bfloat16)


def prepare(n, rotation, row_coefs, col_coefs, row_wedge, col_wedge):
    shape = jax.ShapeDtypeStruct((1, 4 * n, BLOCK), jnp.bfloat16)
    return pl.pallas_call(
        functools.partial(prepare_kernel, n),
        out_shape=[shape, shape],
        in_specs=[pl.BlockSpec(memory_space=pltpu.HBM)] * 5,
        out_specs=[pl.BlockSpec(memory_space=pltpu.VMEM)] * 2,
        scratch_shapes=[pltpu.SMEM((1,), jnp.int32)]
        + [pltpu.VMEM((BLOCK, 2 * ANGLES), jnp.bfloat16)] * 2
        + [pltpu.VMEM((BLOCK,), jnp.int32)] * 2
        + [pltpu.SemaphoreType.DMA((5,))],
        compiler_params=pltpu.CompilerParams(vmem_limit_bytes=8 * 1024 * 1024),
        name="prepare",
    )(rotation, row_coefs.reshape(BLOCK, 2 * ANGLES), col_coefs.reshape(BLOCK, 2 * ANGLES), row_wedge, col_wedge)


STRIPE = 448
FINISH_LIMIT = 16
STRIPES = BLOCK // STRIPE
SIDE = 64


def lanes(j):
    return pl.ds(pl.multiple_of(j * LANES, LANES), LANES)


def wedge_masks(n, rotation_ref, centre, wedge):
    turn = rotation_ref[0] & (HALF - 1)
    r = lax.broadcasted_iota(jnp.int32, (SIDE, LANES), 0)
    bins = kept_bin(r - jnp.where(r >= n, n, 0), turn)
    return jnp.where((r < 2 * n) & wedge_mask(bins, centre, wedge), 1.0, 0.0).astype(jnp.bfloat16)


def energy(n, total):
    both = (total[: 2 * n] + total[2 * n :]).astype(jnp.bfloat16)
    return jnp.concatenate([both, jnp.zeros((SIDE - 2 * n, LANES), jnp.bfloat16)])


def place(wide, slot, block, to):
    rows, deep = block.shape[0], wide.shape[1]
    wide[slot, pl.ds(0, rows), to] = block
    if deep > rows:
        wide[slot, pl.ds(rows, deep - rows), to] = jnp.zeros((deep - rows, LANES), jnp.bfloat16)


def product(a, b):
    return jnp.dot(a, b, preferred_element_type=jnp.float32)


def row_slot(dz, dxh):
    d = dz & 7
    return jnp.where(d == 0, 0, jnp.where(d <= 4, 2 * d - 1, 2 * (8 - d))) * 2 + dxh


def col_slot(dy, dxl, dc):
    me_row, me_col = lax.axis_index("row"), lax.axis_index("col")
    y, xl, c = me_row >> 2, (me_row >> 1) & 1, me_row & 1
    z, xh = me_col >> 1, me_col & 1
    shell = ((y - dy) & 3) * 4 + (xl ^ dxl) * 2 + (c ^ dc)
    return row_slot(z - (shell >> 1), xh ^ (shell & 1))


def gathered(pieces, total, wide, slots, at, to):
    shells = [piece[i, :, at] for piece in pieces for i in range(piece.shape[0])]
    for slot, block in zip(slots, shells):
        place(wide, slot, block, to)
        squares = jnp.square(block.astype(jnp.float32))
        total = squares if total is None else total + squares
    return total


def turned_rows(left, column, at, start):
    wide = column.shape[0] * column.shape[1]
    left[at, pl.ds(start, wide)] = column[...].reshape(wide, LANES).T


def begin_kernel(places, *refs):
    rows, chip = refs[:4], refs[4]
    left, right, row_sums, col_sums, column = refs[5:]
    slots = [col_slot(dy, dxl, 0) for dy, dxl in places]

    def assemble(j, carry):
        at = lanes(j)
        row_sums[:, at] = gathered(rows, None, column, range(8), at, pl.ds(0, LANES))
        turned_rows(left, column, at, 0)
        col_sums[:, at] = gathered([chip], None, right, slots, at, at)
        return carry

    lax.fori_loop(0, BLOCK // LANES, assemble, 0)


def partial_kernel(n, places, rotation_ref, col_wedge_ref, down2, up3, down3, other, early_row_sums, early_col_sums, _, __, left, right, cross_ref, sums_ref, col_masks, col_energies, column):
    deep = right.shape[1]
    start = 8 * deep
    slots = [col_slot(dy, dxl, 1) for dy, dxl in places]
    turn = rotation_ref[0] & (HALF - 1)
    nothing = jnp.zeros((SIDE, LANES), jnp.bfloat16)

    def assemble(j, carry):
        at = lanes(j)
        sums_ref[:, at] = gathered([down2, up3, down3], early_row_sums[:, at], column, range(6), at, pl.ds(0, LANES))
        turned_rows(left, column, at, start)
        total = gathered([other], early_col_sums[:, at], right, slots, at, at)
        col_masks[:, at] = jnp.concatenate([wedge_masks(n, rotation_ref, turn, col_wedge_ref[:, at]), nothing])
        col_energies[:, at] = jnp.concatenate([nothing, energy(n, total)])
        return carry

    lax.fori_loop(0, BLOCK // LANES, assemble, 0)

    def stripe(m, carry):
        at = pl.ds(pl.multiple_of(m * STRIPE, STRIPE), STRIPE)
        cross_ref[at, :] = product(left[at, :], right[: SHELLS - 2].reshape((SHELLS - 2) * deep, BLOCK))
        return carry

    lax.fori_loop(0, STRIPES, stripe, 0, unroll=True)


def finish_kernel(n, rotation_ref, row_wedge_ref, best_ref, cross_ref, sums_ref, right, col_masks, col_energies, first, second, out_ref, column, left, side):
    late = left.shape[1]

    def assemble(j, carry):
        at = lanes(j)
        total = gathered([first, second], sums_ref[:, at], column, range(2), at, pl.ds(0, LANES))
        turned_rows(left, column, at, 0)
        side[at, :] = jnp.concatenate([energy(n, total), wedge_masks(n, rotation_ref, 0, row_wedge_ref[:, at])]).T
        return carry

    lax.fori_loop(0, BLOCK // LANES, assemble, 0)

    def stripe(m, carry):
        at = pl.ds(pl.multiple_of(m * STRIPE, STRIPE), STRIPE)
        cross = cross_ref[at, :] + product(left[at, :], right[SHELLS - 2 :].reshape(late, BLOCK))
        row_norm = product(side[at, :], col_masks[...])
        col_norm = product(side[at, :], col_energies[...])
        score = cross * lax.rsqrt(row_norm * col_norm + 1e-06)
        out_ref[at, :] = jnp.maximum(best_ref[at, :], score)
        return carry

    lax.fori_loop(0, STRIPES, stripe, 0, unroll=True)


SMEM, VMEM = pl.BlockSpec(memory_space=pltpu.SMEM), pl.BlockSpec(memory_space=pltpu.VMEM)
MIB = 1024 * 1024


def begin(n, rows, chip, places):
    deep = -(-4 * n // 16) * 16
    sums = jax.ShapeDtypeStruct((4 * n, BLOCK), jnp.float32)
    return pl.pallas_call(
        functools.partial(begin_kernel, places),
        out_shape=[
            jax.ShapeDtypeStruct((BLOCK, (SHELLS - 2) * deep), jnp.bfloat16),
            jax.ShapeDtypeStruct((SHELLS, deep, BLOCK), jnp.bfloat16),
            sums,
            sums,
        ],
        in_specs=[VMEM] * 5,
        out_specs=[VMEM] * 4,
        scratch_shapes=[pltpu.VMEM((8, deep, LANES), jnp.bfloat16)],
        compiler_params=pltpu.CompilerParams(vmem_limit_bytes=8 * MIB),
        cost_estimate=pl.CostEstimate(flops=16 * 8 * n * BLOCK, bytes_accessed=6 * MIB, transcendentals=0),
        name="begin",
    )(*rows, chip)


def partial_cross(n, rotation, col_wedge, late, other, begun, places):
    left, right, row_sums, col_sums = begun
    deep = right.shape[1]
    sides = jax.ShapeDtypeStruct((2 * SIDE, BLOCK), jnp.bfloat16)
    return pl.pallas_call(
        functools.partial(partial_kernel, n, places),
        out_shape=[
            jax.ShapeDtypeStruct(left.shape, left.dtype),
            jax.ShapeDtypeStruct(right.shape, right.dtype),
            jax.ShapeDtypeStruct((BLOCK, BLOCK), jnp.float32),
            jax.ShapeDtypeStruct((4 * n, BLOCK), jnp.float32),
            sides,
            sides,
        ],
        in_specs=[SMEM] + [VMEM] * 9,
        out_specs=[VMEM] * 6,
        scratch_shapes=[pltpu.VMEM((6, deep, LANES), jnp.bfloat16)],
        input_output_aliases={8: 0, 9: 1},
        compiler_params=pltpu.CompilerParams(vmem_limit_bytes=16 * MIB),
        cost_estimate=pl.CostEstimate(flops=2 * BLOCK * BLOCK * (SHELLS - 2) * deep, bytes_accessed=8 * MIB, transcendentals=0),
        name="partial_cross",
    )(rotation, col_wedge, *late, other, row_sums, col_sums, left, right)


def finish(n, rotation, row_wedge, best_in, cross, sums, right, col_masks, col_energies, last):
    deep = right.shape[1]
    return pl.pallas_call(
        functools.partial(finish_kernel, n),
        out_shape=jax.ShapeDtypeStruct((BLOCK, BLOCK), jnp.float32),
        in_specs=[SMEM] + [VMEM] * 9,
        out_specs=VMEM,
        scratch_shapes=[
            pltpu.VMEM((2, deep, LANES), jnp.bfloat16),
            pltpu.VMEM((BLOCK, 2 * deep), jnp.bfloat16),
            pltpu.VMEM((BLOCK, LANES), jnp.bfloat16),
        ],
        compiler_params=pltpu.CompilerParams(vmem_limit_bytes=FINISH_LIMIT * MIB),
        cost_estimate=pl.CostEstimate(flops=2 * BLOCK * BLOCK * (2 * deep + 4 * SIDE), bytes_accessed=8 * MIB, transcendentals=BLOCK * BLOCK),
        name="finish",
    )(rotation, row_wedge, best_in, cross, sums, right, col_masks, col_energies, *last)


def with_bins(n, row_coefs, col_coefs, row_wedge, col_wedge, rotation, best_in):
    row_own, col_own = prepare(n, rotation, row_coefs, col_coefs, row_wedge, col_wedge)
    row_wedge, col_wedge = row_wedge.reshape(1, BLOCK), col_wedge.reshape(1, BLOCK)
    together = lax.optimization_barrier
    pair = jnp.concatenate([row_own, shift(row_own, dxh=1)])
    col_pair = jnp.concatenate([col_own, shift(col_own, dxl=1)])
    pair, col_pair = together((pair, col_pair))
    up1, down1 = shift(pair, dz=1), shift(pair, dz=-1)
    north, south, across = shift(col_pair, dy=1), shift(col_pair, dy=-1), shift(col_pair, dy=2)
    places = [(dy, dxl) for dy in (0, 1, -1, 2) for dxl in (0, 1)]
    up1, down1 = together((up1, down1))
    up2, down2 = shift(up1, dz=1), shift(down1, dz=-1)
    up2, down2, north, south = together((up2, down2, north, south))
    chip = jnp.concatenate([col_pair, north, south, across])
    up3, down3 = shift(up2, dz=1), shift(down2, dz=-1)
    begun = begin(n, (pair, up1, down1, up2), chip, places)
    up3, down3, chip, begun = together((up3, down3, chip, begun))
    other = shift(chip, dc=1)
    last = (shift(up3[:1], dz=1), shift(down3[1:], dz=-1))
    _, right, cross, sums, masks, energies = partial_cross(n, rotation, col_wedge, (down2, up3, down3), other, begun, places)
    return finish(n, rotation, row_wedge, best_in, cross, sums, right, masks, energies, last)


def shards(row_coefs, col_coefs, row_wedge, col_wedge, rotation, best_in):
    turn = rotation[0] & (HALF - 1)
    apart = jnp.minimum(jnp.minimum(turn, HALF - turn), BAND)
    branches = [functools.partial(with_bins, n) for n in (18, 20, 22, 24, 26)]
    return lax.cond(apart < BAND, functools.partial(with_bins, 26), functools.partial(with_bins, 18), row_coefs, col_coefs, row_wedge, col_wedge, rotation, best_in)


def solution(mesh):
    return jax.shard_map(
        shards,
        mesh=mesh,
        in_specs=(
            P("row", "col", None),
            P("col", "row", None),
            P("row"),
            P("col"),
            P(),
            P("row", "col"),
        ),
        out_specs=P("row", "col"),
        check_vma=False,
    )
```

```python
import functools

import jax
import jax.numpy as jnp
from jax import lax
from jax.experimental import pallas as pl
from jax.experimental.pallas import tpu as pltpu
from jax.sharding import PartitionSpec as P

BLOCK = 896
ANGLES = 64
HALF = 32
SHELLS = 16
NARROWEST = 3
LANES = 128
BAND = 2 * NARROWEST + 1
AXES = ("row", "col")


def coordinates():
    return [(y, xl, c, z, xh) for y in range(4) for xl in range(2) for c in range(2) for z in range(8) for xh in range(2)]


def flat(y, xl, c, z, xh):
    return (y * 4 + xl * 2 + c) * 16 + z * 2 + xh


def shift(x, dy=0, dxl=0, dc=0, dz=0, dxh=0):
    pairs = [
        (flat(y, xl, c, z, xh), flat((y + dy) % 4, (xl + dxl) % 2, (c + dc) % 2, (z + dz) % 8, (xh + dxh) % 2))
        for y, xl, c, z, xh in coordinates()
    ]
    return lax.ppermute(x, AXES, pairs)


def kept_bin(k, turn):
    first = NARROWEST + 1
    low = jnp.maximum(turn - NARROWEST, first)
    skipped = jnp.maximum(turn + NARROWEST + 1 - low, 0)
    place = k + first
    return jnp.where(place < low, place, place + skipped)


def wedge_mask(bins, turn, wedge):
    phase = (bins - turn) & (HALF - 1)
    return jnp.minimum(phase, HALF - phase) > wedge


def prepare_kernel(n, rotation_ref, row_ref, col_ref, row_wedge_ref, col_wedge_ref, row_out, col_out, rotation, row_coefs, col_coefs, row_wedge, col_wedge, sems):
    pairs = (
        (rotation_ref, rotation),
        (row_wedge_ref, row_wedge),
        (row_ref, row_coefs),
        (col_wedge_ref, col_wedge),
        (col_ref, col_coefs),
    )
    loads = [pltpu.make_async_copy(source, target, sems.at[i]) for i, (source, target) in enumerate(pairs)]
    for load in loads:
        load.start()
    loads[0].wait()
    offset = rotation[0] & (ANGLES - 1)
    turn = offset & (HALF - 1)
    rows = 4 * n

    def bins_of(shape):
        r = lax.broadcasted_iota(jnp.int32, shape, 0)
        part = jnp.where(r >= 2 * n, 1, 0)
        r = r - part * (2 * n)
        half = jnp.where(r >= n, 1, 0)
        return part, half, kept_bin(r - half * n, turn)

    part, half, bins = bins_of((rows, 2 * ANGLES))
    feature = lax.broadcasted_iota(jnp.int32, (rows, 2 * ANGLES), 1)
    angle = (bins + HALF * half + HALF // 2) & (ANGLES - 1)
    valid = bins < HALF - NARROWEST
    row_pick = jnp.where(valid & (feature == part * ANGLES + angle), 1.0, 0.0).astype(jnp.bfloat16)
    source = (angle - offset) & (ANGLES - 1)
    col_pick = jnp.where(valid & (feature == part * ANGLES + source), 1.0, 0.0).astype(jnp.bfloat16)
    _, _, bins = bins_of((rows, 1))
    for ready, pick, coefs, wedge, centre, out in (
        (loads[1:3], row_pick, row_coefs, row_wedge, 0, row_out),
        (loads[3:], col_pick, col_coefs, col_wedge, turn, col_out),
    ):
        for load in ready:
            load.wait()
        phase = (bins - centre) & (HALF - 1)
        spread = jnp.minimum(phase, HALF - phase)
        mask = spread > wedge[...].reshape(1, BLOCK)
        picked = lax.dot_general(pick, coefs[...], (((1,), (1,)), ((), ())), preferred_element_type=jnp.float32)
        out[0] = jnp.where(mask, picked, 0.0).astype(jnp.bfloat16)


def prepare(n, rotation, row_coefs, col_coefs, row_wedge, col_wedge):
    shape = jax.ShapeDtypeStruct((1, 4 * n, BLOCK), jnp.bfloat16)
    return pl.pallas_call(
        functools.partial(prepare_kernel, n),
        out_shape=[shape, shape],
        in_specs=[pl.BlockSpec(memory_space=pltpu.HBM)] * 5,
        out_specs=[pl.BlockSpec(memory_space=pltpu.VMEM)] * 2,
        scratch_shapes=[pltpu.SMEM((1,), jnp.int32)]
        + [pltpu.VMEM((BLOCK, 2 * ANGLES), jnp.bfloat16)] * 2
        + [pltpu.VMEM((BLOCK,), jnp.int32)] * 2
        + [pltpu.SemaphoreType.DMA((5,))],
        compiler_params=pltpu.CompilerParams(vmem_limit_bytes=8 * 1024 * 1024),
        name="prepare",
    )(rotation, row_coefs.reshape(BLOCK, 2 * ANGLES), col_coefs.reshape(BLOCK, 2 * ANGLES), row_wedge, col_wedge)


STRIPE = 448
FINISH_LIMIT = 16
STRIPES = BLOCK // STRIPE
SIDE = 64


def lanes(j):
    return pl.ds(pl.multiple_of(j * LANES, LANES), LANES)


def wedge_masks(n, rotation_ref, centre, wedge):
    turn = rotation_ref[0] & (HALF - 1)
    r = lax.broadcasted_iota(jnp.int32, (SIDE, LANES), 0)
    bins = kept_bin(r - jnp.where(r >= n, n, 0), turn)
    return jnp.where((r < 2 * n) & wedge_mask(bins, centre, wedge), 1.0, 0.0).astype(jnp.bfloat16)


def energy(n, total):
    both = (total[: 2 * n] + total[2 * n :]).astype(jnp.bfloat16)
    return jnp.concatenate([both, jnp.zeros((SIDE - 2 * n, LANES), jnp.bfloat16)])


def place(wide, slot, block, to):
    rows, deep = block.shape[0], wide.shape[1]
    wide[slot, pl.ds(0, rows), to] = block
    if deep > rows:
        wide[slot, pl.ds(rows, deep - rows), to] = jnp.zeros((deep - rows, LANES), jnp.bfloat16)


def product(a, b):
    return jnp.dot(a, b, preferred_element_type=jnp.float32)


def row_slot(dz, dxh):
    d = dz & 7
    return jnp.where(d == 0, 0, jnp.where(d <= 4, 2 * d - 1, 2 * (8 - d))) * 2 + dxh


def col_slot(dy, dxl, dc):
    me_row, me_col = lax.axis_index("row"), lax.axis_index("col")
    y, xl, c = me_row >> 2, (me_row >> 1) & 1, me_row & 1
    z, xh = me_col >> 1, me_col & 1
    shell = ((y - dy) & 3) * 4 + (xl ^ dxl) * 2 + (c ^ dc)
    return row_slot(z - (shell >> 1), xh ^ (shell & 1))


def gathered(pieces, total, wide, slots, at, to):
    shells = [piece[i, :, at] for piece in pieces for i in range(piece.shape[0])]
    for slot, block in zip(slots, shells):
        place(wide, slot, block, to)
        squares = jnp.square(block.astype(jnp.float32))
        total = squares if total is None else total + squares
    return total


def turned_rows(left, column, at, start):
    wide = column.shape[0] * column.shape[1]
    left[at, pl.ds(start, wide)] = column[...].reshape(wide, LANES).T


def begin_kernel(places, *refs):
    rows, chip = refs[:4], refs[4]
    left, right, row_sums, col_sums, column = refs[5:]
    slots = [col_slot(dy, dxl, 0) for dy, dxl in places]

    def assemble(j, carry):
        at = lanes(j)
        row_sums[:, at] = gathered(rows, None, column, range(8), at, pl.ds(0, LANES))
        turned_rows(left, column, at, 0)
        col_sums[:, at] = gathered([chip], None, right, slots, at, at)
        return carry

    lax.fori_loop(0, BLOCK // LANES, assemble, 0)


def partial_kernel(n, places, rotation_ref, col_wedge_ref, down2, up3, down3, other, early_row_sums, early_col_sums, _, __, left, right, cross_ref, sums_ref, col_masks, col_energies, column):
    deep = right.shape[1]
    start = 8 * deep
    slots = [col_slot(dy, dxl, 1) for dy, dxl in places]
    turn = rotation_ref[0] & (HALF - 1)
    nothing = jnp.zeros((SIDE, LANES), jnp.bfloat16)

    def assemble(j, carry):
        at = lanes(j)
        sums_ref[:, at] = gathered([down2, up3, down3], early_row_sums[:, at], column, range(6), at, pl.ds(0, LANES))
        turned_rows(left, column, at, start)
        total = gathered([other], early_col_sums[:, at], right, slots, at, at)
        col_masks[:, at] = jnp.concatenate([wedge_masks(n, rotation_ref, turn, col_wedge_ref[:, at]), nothing])
        col_energies[:, at] = jnp.concatenate([nothing, energy(n, total)])
        return carry

    lax.fori_loop(0, BLOCK // LANES, assemble, 0)

    def stripe(m, carry):
        at = pl.ds(pl.multiple_of(m * STRIPE, STRIPE), STRIPE)
        cross_ref[at, :] = product(left[at, :], right[: SHELLS - 2].reshape((SHELLS - 2) * deep, BLOCK))
        return carry

    lax.fori_loop(0, STRIPES, stripe, 0, unroll=True)


def finish_kernel(n, rotation_ref, row_wedge_ref, best_ref, cross_ref, sums_ref, right, col_masks, col_energies, first, second, out_ref, column, left, side):
    late = left.shape[1]

    def assemble(j, carry):
        at = lanes(j)
        total = gathered([first, second], sums_ref[:, at], column, range(2), at, pl.ds(0, LANES))
        turned_rows(left, column, at, 0)
        side[at, :] = jnp.concatenate([energy(n, total), wedge_masks(n, rotation_ref, 0, row_wedge_ref[:, at])]).T
        return carry

    lax.fori_loop(0, BLOCK // LANES, assemble, 0)

    def stripe(m, carry):
        at = pl.ds(pl.multiple_of(m * STRIPE, STRIPE), STRIPE)
        cross = cross_ref[at, :] + product(left[at, :], right[SHELLS - 2 :].reshape(late, BLOCK))
        row_norm = product(side[at, :], col_masks[...])
        col_norm = product(side[at, :], col_energies[...])
        score = cross * lax.rsqrt(row_norm * col_norm + 1e-06)
        out_ref[at, :] = jnp.maximum(best_ref[at, :], score)
        return carry

    lax.fori_loop(0, STRIPES, stripe, 0, unroll=True)


SMEM, VMEM = pl.BlockSpec(memory_space=pltpu.SMEM), pl.BlockSpec(memory_space=pltpu.VMEM)
MIB = 1024 * 1024


def begin(n, rows, chip, places):
    deep = -(-4 * n // 16) * 16
    sums = jax.ShapeDtypeStruct((4 * n, BLOCK), jnp.float32)
    return pl.pallas_call(
        functools.partial(begin_kernel, places),
        out_shape=[
            jax.ShapeDtypeStruct((BLOCK, (SHELLS - 2) * deep), jnp.bfloat16),
            jax.ShapeDtypeStruct((SHELLS, deep, BLOCK), jnp.bfloat16),
            sums,
            sums,
        ],
        in_specs=[VMEM] * 5,
        out_specs=[VMEM] * 4,
        scratch_shapes=[pltpu.VMEM((8, deep, LANES), jnp.bfloat16)],
        compiler_params=pltpu.CompilerParams(vmem_limit_bytes=8 * MIB),
        cost_estimate=pl.CostEstimate(flops=16 * 8 * n * BLOCK, bytes_accessed=6 * MIB, transcendentals=0),
        name="begin",
    )(*rows, chip)


def partial_cross(n, rotation, col_wedge, late, other, begun, places):
    left, right, row_sums, col_sums = begun
    deep = right.shape[1]
    sides = jax.ShapeDtypeStruct((2 * SIDE, BLOCK), jnp.bfloat16)
    return pl.pallas_call(
        functools.partial(partial_kernel, n, places),
        out_shape=[
            jax.ShapeDtypeStruct(left.shape, left.dtype),
            jax.ShapeDtypeStruct(right.shape, right.dtype),
            jax.ShapeDtypeStruct((BLOCK, BLOCK), jnp.float32),
            jax.ShapeDtypeStruct((4 * n, BLOCK), jnp.float32),
            sides,
            sides,
        ],
        in_specs=[SMEM] + [VMEM] * 9,
        out_specs=[VMEM] * 6,
        scratch_shapes=[pltpu.VMEM((6, deep, LANES), jnp.bfloat16)],
        input_output_aliases={8: 0, 9: 1},
        compiler_params=pltpu.CompilerParams(vmem_limit_bytes=16 * MIB),
        cost_estimate=pl.CostEstimate(flops=2 * BLOCK * BLOCK * (SHELLS - 2) * deep, bytes_accessed=8 * MIB, transcendentals=0),
        name="partial_cross",
    )(rotation, col_wedge, *late, other, row_sums, col_sums, left, right)


def finish(n, rotation, row_wedge, best_in, cross, sums, right, col_masks, col_energies, last):
    deep = right.shape[1]
    return pl.pallas_call(
        functools.partial(finish_kernel, n),
        out_shape=jax.ShapeDtypeStruct((BLOCK, BLOCK), jnp.float32),
        in_specs=[SMEM] + [VMEM] * 9,
        out_specs=VMEM,
        scratch_shapes=[
            pltpu.VMEM((2, deep, LANES), jnp.bfloat16),
            pltpu.VMEM((BLOCK, 2 * deep), jnp.bfloat16),
            pltpu.VMEM((BLOCK, LANES), jnp.bfloat16),
        ],
        compiler_params=pltpu.CompilerParams(vmem_limit_bytes=FINISH_LIMIT * MIB),
        cost_estimate=pl.CostEstimate(flops=2 * BLOCK * BLOCK * (2 * deep + 4 * SIDE), bytes_accessed=8 * MIB, transcendentals=BLOCK * BLOCK),
        name="finish",
    )(rotation, row_wedge, best_in, cross, sums, right, col_masks, col_energies, *last)


def with_bins(n, row_coefs, col_coefs, row_wedge, col_wedge, rotation, best_in):
    row_own, col_own = prepare(n, rotation, row_coefs, col_coefs, row_wedge, col_wedge)
    row_wedge, col_wedge = row_wedge.reshape(1, BLOCK), col_wedge.reshape(1, BLOCK)
    together = lax.optimization_barrier
    pair = jnp.concatenate([row_own, shift(row_own, dxh=1)])
    pair, col_own = together((pair, col_own))
    up1, down1 = shift(pair, dz=1), shift(pair, dz=-1)
    col_pair = jnp.concatenate([col_own, shift(col_own, dxl=1)])
    up1, down1, col_pair = together((up1, down1, col_pair))
    up2, down2 = shift(up1, dz=1), shift(down1, dz=-1)
    north, south, across = shift(col_pair, dy=1), shift(col_pair, dy=-1), shift(col_pair, dy=2)
    places = [(dy, dxl) for dy in (0, 1, -1, 2) for dxl in (0, 1)]
    up2, down2 = together((up2, down2))
    chip = jnp.concatenate([col_pair, north, south, across])
    up3, down3 = shift(up2, dz=1), shift(down2, dz=-1)
    begun = begin(n, (pair, up1, down1, up2), chip, places)
    up3, down3, chip, begun = together((up3, down3, chip, begun))
    other = shift(chip, dc=1)
    last = (shift(up3[:1], dz=1), shift(down3[1:], dz=-1))
    _, right, cross, sums, masks, energies = partial_cross(n, rotation, col_wedge, (down2, up3, down3), other, begun, places)
    return finish(n, rotation, row_wedge, best_in, cross, sums, right, masks, energies, last)


def shards(row_coefs, col_coefs, row_wedge, col_wedge, rotation, best_in):
    turn = rotation[0] & (HALF - 1)
    apart = jnp.minimum(jnp.minimum(turn, HALF - turn), BAND)
    branches = [functools.partial(with_bins, n) for n in (18, 20, 22, 24, 26)]
    return lax.cond(apart < BAND, functools.partial(with_bins, 26), functools.partial(with_bins, 18), row_coefs, col_coefs, row_wedge, col_wedge, rotation, best_in)


def solution(mesh):
    return jax.shard_map(
        shards,
        mesh=mesh,
        in_specs=(
            P("row", "col", None),
            P("col", "row", None),
            P("row"),
            P("col"),
            P(),
            P("row", "col"),
        ),
        out_specs=P("row", "col"),
        check_vma=False,
    )
```

```python
import functools

import jax
import jax.numpy as jnp
from jax import lax
from jax.experimental import pallas as pl
from jax.experimental.pallas import tpu as pltpu
from jax.sharding import PartitionSpec as P

BLOCK = 896
ANGLES = 64
HALF = 32
SHELLS = 16
NARROWEST = 3
LANES = 128
BAND = 2 * NARROWEST + 1
AXES = ("row", "col")


def coordinates():
    return [(y, xl, c, z, xh) for y in range(4) for xl in range(2) for c in range(2) for z in range(8) for xh in range(2)]


def flat(y, xl, c, z, xh):
    return (y * 4 + xl * 2 + c) * 16 + z * 2 + xh


def shift(x, dy=0, dxl=0, dc=0, dz=0, dxh=0):
    pairs = [
        (flat(y, xl, c, z, xh), flat((y + dy) % 4, (xl + dxl) % 2, (c + dc) % 2, (z + dz) % 8, (xh + dxh) % 2))
        for y, xl, c, z, xh in coordinates()
    ]
    return lax.ppermute(x, AXES, pairs)


def kept_bin(k, turn):
    first = NARROWEST + 1
    low = jnp.maximum(turn - NARROWEST, first)
    skipped = jnp.maximum(turn + NARROWEST + 1 - low, 0)
    place = k + first
    return jnp.where(place < low, place, place + skipped)


def wedge_mask(bins, turn, wedge):
    phase = (bins - turn) & (HALF - 1)
    return jnp.minimum(phase, HALF - phase) > wedge


def prepare_kernel(n, rotation_ref, row_ref, col_ref, row_wedge_ref, col_wedge_ref, row_out, col_out, rotation, row_coefs, col_coefs, row_wedge, col_wedge, sems):
    pairs = (
        (rotation_ref, rotation),
        (row_wedge_ref, row_wedge),
        (row_ref, row_coefs),
        (col_wedge_ref, col_wedge),
        (col_ref, col_coefs),
    )
    loads = [pltpu.make_async_copy(source, target, sems.at[i]) for i, (source, target) in enumerate(pairs)]
    for load in loads:
        load.start()
    loads[0].wait()
    offset = rotation[0] & (ANGLES - 1)
    turn = offset & (HALF - 1)
    rows = 4 * n

    def bins_of(shape):
        r = lax.broadcasted_iota(jnp.int32, shape, 0)
        part = jnp.where(r >= 2 * n, 1, 0)
        r = r - part * (2 * n)
        half = jnp.where(r >= n, 1, 0)
        return part, half, kept_bin(r - half * n, turn)

    part, half, bins = bins_of((rows, 2 * ANGLES))
    feature = lax.broadcasted_iota(jnp.int32, (rows, 2 * ANGLES), 1)
    angle = (bins + HALF * half + HALF // 2) & (ANGLES - 1)
    valid = bins < HALF - NARROWEST
    row_pick = jnp.where(valid & (feature == part * ANGLES + angle), 1.0, 0.0).astype(jnp.bfloat16)
    source = (angle - offset) & (ANGLES - 1)
    col_pick = jnp.where(valid & (feature == part * ANGLES + source), 1.0, 0.0).astype(jnp.bfloat16)
    _, _, bins = bins_of((rows, 1))
    for ready, pick, coefs, wedge, centre, out in (
        (loads[1:3], row_pick, row_coefs, row_wedge, 0, row_out),
        (loads[3:], col_pick, col_coefs, col_wedge, turn, col_out),
    ):
        for load in ready:
            load.wait()
        phase = (bins - centre) & (HALF - 1)
        spread = jnp.minimum(phase, HALF - phase)
        mask = spread > wedge[...].reshape(1, BLOCK)
        picked = lax.dot_general(pick, coefs[...], (((1,), (1,)), ((), ())), preferred_element_type=jnp.float32)
        out[0] = jnp.where(mask, picked, 0.0).astype(jnp.bfloat16)


def prepare(n, rotation, row_coefs, col_coefs, row_wedge, col_wedge):
    shape = jax.ShapeDtypeStruct((1, 4 * n, BLOCK), jnp.bfloat16)
    return pl.pallas_call(
        functools.partial(prepare_kernel, n),
        out_shape=[shape, shape],
        in_specs=[pl.BlockSpec(memory_space=pltpu.HBM)] * 5,
        out_specs=[pl.BlockSpec(memory_space=pltpu.VMEM)] * 2,
        scratch_shapes=[pltpu.SMEM((1,), jnp.int32)]
        + [pltpu.VMEM((BLOCK, 2 * ANGLES), jnp.bfloat16)] * 2
        + [pltpu.VMEM((BLOCK,), jnp.int32)] * 2
        + [pltpu.SemaphoreType.DMA((5,))],
        compiler_params=pltpu.CompilerParams(vmem_limit_bytes=8 * 1024 * 1024),
        name="prepare",
    )(rotation, row_coefs.reshape(BLOCK, 2 * ANGLES), col_coefs.reshape(BLOCK, 2 * ANGLES), row_wedge, col_wedge)


STRIPE = 448
FINISH_LIMIT = 16
STRIPES = BLOCK // STRIPE
SIDE = 64


def lanes(j):
    return pl.ds(pl.multiple_of(j * LANES, LANES), LANES)


def wedge_masks(n, rotation_ref, centre, wedge):
    turn = rotation_ref[0] & (HALF - 1)
    r = lax.broadcasted_iota(jnp.int32, (SIDE, LANES), 0)
    bins = kept_bin(r - jnp.where(r >= n, n, 0), turn)
    return jnp.where((r < 2 * n) & wedge_mask(bins, centre, wedge), 1.0, 0.0).astype(jnp.bfloat16)


def energy(n, total):
    both = (total[: 2 * n] + total[2 * n :]).astype(jnp.bfloat16)
    return jnp.concatenate([both, jnp.zeros((SIDE - 2 * n, LANES), jnp.bfloat16)])


def place(wide, slot, block, to):
    rows, deep = block.shape[0], wide.shape[1]
    wide[slot, pl.ds(0, rows), to] = block
    if deep > rows:
        wide[slot, pl.ds(rows, deep - rows), to] = jnp.zeros((deep - rows, LANES), jnp.bfloat16)


def product(a, b):
    return jnp.dot(a, b, preferred_element_type=jnp.float32)


def row_slot(dz, dxh):
    d = dz & 7
    return jnp.where(d == 0, 0, jnp.where(d <= 4, 2 * d - 1, 2 * (8 - d))) * 2 + dxh


def col_slot(dy, dxl, dc):
    me_row, me_col = lax.axis_index("row"), lax.axis_index("col")
    y, xl, c = me_row >> 2, (me_row >> 1) & 1, me_row & 1
    z, xh = me_col >> 1, me_col & 1
    shell = ((y - dy) & 3) * 4 + (xl ^ dxl) * 2 + (c ^ dc)
    return row_slot(z - (shell >> 1), xh ^ (shell & 1))


def gathered(pieces, total, wide, slots, at, to):
    shells = [piece[i, :, at] for piece in pieces for i in range(piece.shape[0])]
    for slot, block in zip(slots, shells):
        place(wide, slot, block, to)
        squares = jnp.square(block.astype(jnp.float32))
        total = squares if total is None else total + squares
    return total


def turned_rows(left, column, at, start):
    wide = column.shape[0] * column.shape[1]
    left[at, pl.ds(start, wide)] = column[...].reshape(wide, LANES).T


def begin_kernel(places, *refs):
    rows, cols = refs[:4], refs[4:7]
    left, right, row_sums, col_sums, column = refs[7:]
    slots = [col_slot(dy, dxl, 0) for dy, dxl in places[:6]]

    def assemble(j, carry):
        at = lanes(j)
        row_sums[:, at] = gathered(rows, None, column, range(8), at, pl.ds(0, LANES))
        turned_rows(left, column, at, 0)
        col_sums[:, at] = gathered(cols, None, right, slots, at, at)
        return carry

    lax.fori_loop(0, BLOCK // LANES, assemble, 0)


def partial_kernel(n, places, rotation_ref, col_wedge_ref, down2, up3, down3, across, other, early_row_sums, early_col_sums, _, __, left, right, cross_ref, sums_ref, col_masks, col_energies, column):
    deep = right.shape[1]
    start = 8 * deep
    slots = [col_slot(dy, dxl, 0) for dy, dxl in places[6:]] + [col_slot(dy, dxl, 1) for dy, dxl in places]
    turn = rotation_ref[0] & (HALF - 1)
    nothing = jnp.zeros((SIDE, LANES), jnp.bfloat16)

    def assemble(j, carry):
        at = lanes(j)
        sums_ref[:, at] = gathered([down2, up3, down3], early_row_sums[:, at], column, range(6), at, pl.ds(0, LANES))
        turned_rows(left, column, at, start)
        total = gathered([across, other], early_col_sums[:, at], right, slots, at, at)
        col_masks[:, at] = jnp.concatenate([wedge_masks(n, rotation_ref, turn, col_wedge_ref[:, at]), nothing])
        col_energies[:, at] = jnp.concatenate([nothing, energy(n, total)])
        return carry

    lax.fori_loop(0, BLOCK // LANES, assemble, 0)

    def stripe(m, carry):
        at = pl.ds(pl.multiple_of(m * STRIPE, STRIPE), STRIPE)
        cross_ref[at, :] = product(left[at, :], right[: SHELLS - 2].reshape((SHELLS - 2) * deep, BLOCK))
        return carry

    lax.fori_loop(0, STRIPES, stripe, 0, unroll=True)


def finish_kernel(n, rotation_ref, row_wedge_ref, best_ref, cross_ref, sums_ref, right, col_masks, col_energies, first, second, out_ref, column, left, side):
    late = left.shape[1]

    def assemble(j, carry):
        at = lanes(j)
        total = gathered([first, second], sums_ref[:, at], column, range(2), at, pl.ds(0, LANES))
        turned_rows(left, column, at, 0)
        side[at, :] = jnp.concatenate([energy(n, total), wedge_masks(n, rotation_ref, 0, row_wedge_ref[:, at])]).T
        return carry

    lax.fori_loop(0, BLOCK // LANES, assemble, 0)

    def stripe(m, carry):
        at = pl.ds(pl.multiple_of(m * STRIPE, STRIPE), STRIPE)
        cross = cross_ref[at, :] + product(left[at, :], right[SHELLS - 2 :].reshape(late, BLOCK))
        row_norm = product(side[at, :], col_masks[...])
        col_norm = product(side[at, :], col_energies[...])
        score = cross * lax.rsqrt(row_norm * col_norm + 1e-06)
        out_ref[at, :] = jnp.maximum(best_ref[at, :], score)
        return carry

    lax.fori_loop(0, STRIPES, stripe, 0, unroll=True)


SMEM, VMEM = pl.BlockSpec(memory_space=pltpu.SMEM), pl.BlockSpec(memory_space=pltpu.VMEM)
MIB = 1024 * 1024


def begin(n, rows, cols, places):
    deep = -(-4 * n // 16) * 16
    sums = jax.ShapeDtypeStruct((4 * n, BLOCK), jnp.float32)
    return pl.pallas_call(
        functools.partial(begin_kernel, places),
        out_shape=[
            jax.ShapeDtypeStruct((BLOCK, (SHELLS - 2) * deep), jnp.bfloat16),
            jax.ShapeDtypeStruct((SHELLS, deep, BLOCK), jnp.bfloat16),
            sums,
            sums,
        ],
        in_specs=[VMEM] * 7,
        out_specs=[VMEM] * 4,
        scratch_shapes=[pltpu.VMEM((8, deep, LANES), jnp.bfloat16)],
        compiler_params=pltpu.CompilerParams(vmem_limit_bytes=8 * MIB),
        cost_estimate=pl.CostEstimate(flops=16 * 8 * n * BLOCK, bytes_accessed=6 * MIB, transcendentals=0),
        name="begin",
    )(*rows, *cols)


def partial_cross(n, rotation, col_wedge, late, across, other, begun, places):
    left, right, row_sums, col_sums = begun
    deep = right.shape[1]
    sides = jax.ShapeDtypeStruct((2 * SIDE, BLOCK), jnp.bfloat16)
    return pl.pallas_call(
        functools.partial(partial_kernel, n, places),
        out_shape=[
            jax.ShapeDtypeStruct(left.shape, left.dtype),
            jax.ShapeDtypeStruct(right.shape, right.dtype),
            jax.ShapeDtypeStruct((BLOCK, BLOCK), jnp.float32),
            jax.ShapeDtypeStruct((4 * n, BLOCK), jnp.float32),
            sides,
            sides,
        ],
        in_specs=[SMEM] + [VMEM] * 10,
        out_specs=[VMEM] * 6,
        scratch_shapes=[pltpu.VMEM((6, deep, LANES), jnp.bfloat16)],
        input_output_aliases={9: 0, 10: 1},
        compiler_params=pltpu.CompilerParams(vmem_limit_bytes=16 * MIB),
        cost_estimate=pl.CostEstimate(flops=2 * BLOCK * BLOCK * (SHELLS - 2) * deep, bytes_accessed=8 * MIB, transcendentals=0),
        name="partial_cross",
    )(rotation, col_wedge, *late, across, other, row_sums, col_sums, left, right)


def finish(n, rotation, row_wedge, best_in, cross, sums, right, col_masks, col_energies, last):
    deep = right.shape[1]
    return pl.pallas_call(
        functools.partial(finish_kernel, n),
        out_shape=jax.ShapeDtypeStruct((BLOCK, BLOCK), jnp.float32),
        in_specs=[SMEM] + [VMEM] * 9,
        out_specs=VMEM,
        scratch_shapes=[
            pltpu.VMEM((2, deep, LANES), jnp.bfloat16),
            pltpu.VMEM((BLOCK, 2 * deep), jnp.bfloat16),
            pltpu.VMEM((BLOCK, LANES), jnp.bfloat16),
        ],
        compiler_params=pltpu.CompilerParams(vmem_limit_bytes=FINISH_LIMIT * MIB),
        cost_estimate=pl.CostEstimate(flops=2 * BLOCK * BLOCK * (2 * deep + 4 * SIDE), bytes_accessed=8 * MIB, transcendentals=BLOCK * BLOCK),
        name="finish",
    )(rotation, row_wedge, best_in, cross, sums, right, col_masks, col_energies, *last)


def with_bins(n, row_coefs, col_coefs, row_wedge, col_wedge, rotation, best_in):
    row_own, col_own = prepare(n, rotation, row_coefs, col_coefs, row_wedge, col_wedge)
    row_wedge, col_wedge = row_wedge.reshape(1, BLOCK), col_wedge.reshape(1, BLOCK)
    together = lax.optimization_barrier
    pair = jnp.concatenate([row_own, shift(row_own, dxh=1)])
    pair, col_own = together((pair, col_own))
    up1, down1 = shift(pair, dz=1), shift(pair, dz=-1)
    col_pair = jnp.concatenate([col_own, shift(col_own, dxl=1)])
    up1, down1, col_pair = together((up1, down1, col_pair))
    up2, down2 = shift(up1, dz=1), shift(down1, dz=-1)
    north, south, across = shift(col_pair, dy=1), shift(col_pair, dy=-1), shift(col_pair, dy=2)
    places = [(dy, dxl) for dy in (0, 1, -1, 2) for dxl in (0, 1)]
    up2, down2 = together((up2, down2))
    chip = jnp.concatenate([col_pair, north, south, across])
    up3, down3 = shift(up2, dz=1), shift(down2, dz=-1)
    begun = begin(n, (pair, up1, down1, up2), (col_pair, north, south), places)
    up3, down3, chip, begun = together((up3, down3, chip, begun))
    other = shift(chip, dc=1)
    last = (shift(up3[:1], dz=1), shift(down3[1:], dz=-1))
    _, right, cross, sums, masks, energies = partial_cross(n, rotation, col_wedge, (down2, up3, down3), across, other, begun, places)
    return finish(n, rotation, row_wedge, best_in, cross, sums, right, masks, energies, last)


def shards(row_coefs, col_coefs, row_wedge, col_wedge, rotation, best_in):
    turn = rotation[0] & (HALF - 1)
    apart = jnp.minimum(jnp.minimum(turn, HALF - turn), BAND)
    branches = [functools.partial(with_bins, n) for n in (18, 20, 22, 24, 26)]
    return lax.cond(apart < BAND, functools.partial(with_bins, 26), functools.partial(with_bins, 18), row_coefs, col_coefs, row_wedge, col_wedge, rotation, best_in)


def solution(mesh):
    return jax.shard_map(
        shards,
        mesh=mesh,
        in_specs=(
            P("row", "col", None),
            P("col", "row", None),
            P("row"),
            P("col"),
            P(),
            P("row", "col"),
        ),
        out_specs=P("row", "col"),
        check_vma=False,
    )
```
